256 devices in a mesh: pole: 4 (over y), row: 8 (over z_lo, core), col: 8 (over x, z_hi).
Axes of the slice: x: 4, y: 4, z: 8 (z_hi: 2, z_lo: 4; z = z_hi * 4 + z_lo), core: 2. Of those that a mesh axis runs over, the one named last changes fastest.
Arguments:
- inverse_tiles: float32 [8, 2, 8, 512, 4096], P('pole', None, None, 'col', 'row'), may hold values from -6 to 6
- factor_block: float32 [8, 2, 4096, 512], P('pole', None, ('row', 'col')), may hold values from -0.09375 to 0.09375
- diag_inverse: float32 [8, 2, 2, 256, 256], P('pole'), may hold values from -6 to 6
- tile_pattern: int32 [64, 64], replicated, may hold values 0 or 1
- ancestor_blocks: int32 [2, 64], replicated, may hold values 0 or 1
- row_owner: int32 [4096, 1], P(('row', 'col')), may hold values from 0 to 3; in each aligned block of 64 rows (0 to 63, 64 to 127, ...) at most 32 rows name the same one
- pole_weights: float32 [8, 2], replicated, may hold values from -4 to 4
- pole_order: int32 [8], replicated, may hold values from 0 to 7, each once
Outputs:
- inverse_rows: float32 [8, 2, 4096, 512], P('pole', None, ('row', 'col'))
- owned_density: float32 [4, 2048, 512], P('pole', ('row', 'col'))
- block_density: float32 [2, 256, 256], replicated
The draws below stay inside these ranges and needn't reach their ends.
Inputs may be any that keep to these rules, and one draw needn't show every extreme that they name: `row_owner`: in each aligned block of 64 rows (the rows of one device) no owner has more than 32 rows, and some owner has exactly 32 in some block.
All inputs are finite; a program needn't handle non-finite values.
Results may differ from the reference program's by a relative error of at most 0.000073.
Values sent between devices are 32-bit elements; how exact they have to be, the bound alone decides.
A program may use at most 64 MiB of HBM per device.

```python
import math
import jax
import jax.numpy as jnp
import numpy as np
from jax import lax

S = 256
NSUP = 2
NA = 4096
POLES = 8
W = 512
NB = 64
BLK = 64
SEGR = 512
CAP = 32
N_POLE = 4
N_ROW = 8


def plant(drawn, stream_key, low, high):
    place = [jax.random.randint(jax.random.fold_in(stream_key, axis), (), 0, length) for axis, length in enumerate(drawn.shape)]
    longest = drawn.shape.index(max(drawn.shape))
    neighbour = place[:longest] + [(place[longest] + 1) % drawn.shape[longest]] + place[longest + 1:]
    return drawn.at[tuple(place)].set(low).at[tuple(neighbour)].set(high)


def levels(key, extent, cuts, least, high):
    def one(axis_at, blocks):
        steps = jax.random.uniform(jax.random.fold_in(jax.random.fold_in(key, 6), axis_at), (blocks,), jnp.float32, least / len(cuts), high / len(cuts))
        return jnp.repeat(jnp.exp(steps), extent[axis_at] // blocks).reshape((-1,) + (1,) * (len(extent) - axis_at - 1))

    factor_of = one(*cuts[0])
    for cut in cuts[1:]:
        factor_of = factor_of * one(*cut)
    return factor_of


def shared_out(key, own, number, rows, amount, top, reach, lean):
    order = jax.random.permutation(key, amount)
    crowded, common = portions_of(amount, rows * top, reach, lean, True), portions_of(amount, rows * top, reach, lean, False)
    places = jnp.arange(amount)

    def named(sizes, rotation):
        used = int((sizes > 0).sum())
        fixed = max(1, used // 4)
        passed = fixed + (places - fixed + rotation * (used - fixed)) % max(1, amount - fixed)
        return jnp.zeros((amount,), jnp.int32).at[order[jnp.where(places < fixed, places, passed)]].set(jnp.asarray(sizes, jnp.int32))

    sizes = jnp.where(number % 4 == 0, named(crowded, number // 4), named(common, number - number // 4 - 1))
    mixed = jax.random.permutation(jax.random.fold_in(own, 3), amount)
    source_of, sink = mixed[0:amount // 2 * 2:2], mixed[1:amount // 2 * 2:2]
    room = jnp.minimum(sizes[source_of] - 1, reach - sizes[sink]) // 2
    room = jnp.where((source_of == order[0]) | (sink == order[0]) | (sizes[sink] == 0), 0, jnp.maximum(room, 0))
    passed = jax.random.randint(jax.random.fold_in(own, 4), (amount // 2,), 0, 1 << 20) % (room + 1)
    sizes = sizes.at[source_of].add(-passed).at[sink].add(passed)
    items = jnp.searchsorted(jnp.cumsum(sizes), jnp.arange(rows * top), side="right").astype(jnp.int32)
    grid = items.reshape(top, rows).T
    grid = grid[jax.random.permutation(jax.random.fold_in(own, 1), rows)]
    rotation = jax.random.randint(jax.random.fold_in(own, 2), (rows, 1), 0, top)
    return jnp.take_along_axis(grid, (jnp.arange(top)[None, :] + rotation) % top, axis=1)


def portions_of(amount, total, most, skew, full):
    loads = [(1 << 20) // math.isqrt(standing ** skew) + 1 for standing in range(1, amount + 1)]
    largest = most if full else min(most, max(-(-total // amount), total * loads[0] // sum(loads)))
    least = 1 if total - largest >= amount - 1 else 0
    counts, rest = [largest] + [least] * (amount - 1), total - largest - least * (amount - 1)
    while rest > 0:
        free = [i for i in range(1, amount) if counts[i] < largest] or [i for i in range(1, amount) if counts[i] < most]
        whole, budget = sum([loads[i] for i in free]), rest
        for i in free:
            addition = min(most - counts[i], max(1, budget * loads[i] // whole), rest)
            counts[i] = counts[i] + addition
            rest = rest - addition
    return np.array(counts)


def scatter_about(rng, dims, deviation, limit, cuts=(), kind=jnp.bfloat16):
    factor_of = levels(rng, dims, cuts, -0.22, 0.18) if cuts else 1.0
    values = jax.random.normal(rng, dims, jnp.float32) * deviation * factor_of
    return jnp.minimum(jnp.maximum(values, -limit), limit).astype(kind)


def setup_inputs(seed: int = 0) -> dict:
    key_list = jax.random.split(jax.random.key(seed), 9)
    inverse_tiles = scatter_about(key_list[0], (POLES, 2, N_ROW, SEGR, NA), 1.0, 6.0, ((0, 4), (3, 8), (4, 8)), jnp.float32)
    factor_block = scatter_about(key_list[1], (POLES, 2, NA, W), NA ** -0.5, 0.09375, ((0, 4), (2, 64)), jnp.float32)
    diag_inverse = scatter_about(key_list[2], (POLES, 2, NSUP, S, S), 1.0, 6.0, ((0, 4),), jnp.float32)
    tile_pattern = plant((jax.random.randint(key_list[3], (NB, NB), 0, 4) < 3).astype(jnp.int32), jax.random.fold_in(key_list[3], 1), 0, 1)
    ancestor_blocks = plant((jax.random.randint(key_list[4], (NSUP, NB), 0, 2) < 1).astype(jnp.int32), jax.random.fold_in(key_list[4], 1), 0, 1)
    row_owner_keys = jax.random.split(jax.random.fold_in(key_list[5], 1), NA // BLK)
    row_owner_turns = jax.random.permutation(jax.random.fold_in(key_list[5], 3), NA // BLK)
    row_owner = jax.vmap(lambda own, number: shared_out(jax.random.fold_in(key_list[5], 2), own, number, BLK, N_POLE, 1, CAP, 2))(row_owner_keys, row_owner_turns).reshape((NA, 1))
    pole_weights = scatter_about(key_list[6], (POLES, 2), 1.0, 4.0, (), jnp.float32)
    pole_order = jax.random.permutation(key_list[7], POLES).astype(jnp.int32)
    return {"inverse_tiles": inverse_tiles, "factor_block": factor_block, "diag_inverse": diag_inverse, "tile_pattern": tile_pattern, "ancestor_blocks": ancestor_blocks, "row_owner": row_owner, "pole_weights": pole_weights, "pole_order": pole_order}


def matmul_high(left, right):
    return jnp.dot(left, right, precision=lax.Precision.HIGHEST, preferred_element_type=jnp.float32)


def reference(inverse_tiles, factor_block, diag_inverse, tile_pattern, ancestor_blocks, row_owner, pole_weights, pole_order):
    tile_full = jnp.repeat(jnp.repeat(tile_pattern.astype(jnp.float32), BLK, axis=0), BLK, axis=1)
    keep_rows = jnp.repeat(jnp.repeat(ancestor_blocks.T.astype(jnp.float32), BLK, axis=0), S, axis=1)

    def pole_solve(packed):
        inv_part, fac_part, diag_part = packed
        matrix = inv_part.reshape(2, NA, NA) * tile_full
        factor = fac_part * keep_rows
        real_part = matmul_high(matrix[0], factor[0]) - matmul_high(matrix[1], factor[1])
        imag_part = matmul_high(matrix[0], factor[1]) + matmul_high(matrix[1], factor[0])
        rows_real = real_part * keep_rows
        rows_imag = imag_part * keep_rows
        fac_real = factor[0].reshape(NA, NSUP, S)
        fac_imag = factor[1].reshape(NA, NSUP, S)
        yr_split = rows_real.reshape(NA, NSUP, S)
        yi_split = rows_imag.reshape(NA, NSUP, S)

        def contract(first, second):
            return jnp.einsum("aks,akt->kst", first, second, precision=lax.Precision.HIGHEST)

        prod_real = contract(fac_real, yr_split) - contract(fac_imag, yi_split)
        prod_imag = contract(fac_real, yi_split) + contract(fac_imag, yr_split)
        green = jnp.stack([diag_part[0] - prod_real, diag_part[1] - prod_imag], axis=0)
        return jnp.stack([rows_real, rows_imag], axis=0), green

    inverse_rows, green_all = lax.map(pole_solve, (inverse_tiles, factor_block, diag_inverse))
    one_hot = (pole_order[:, None] == jnp.arange(POLES, dtype=jnp.int32)[None, :]).astype(jnp.float32)
    weights = matmul_high(one_hot, pole_weights)
    weight_real = weights[:, 0]
    weight_imag = weights[:, 1]
    block_density = jnp.sum(weight_real[:, None, None, None] * green_all[:, 1] + weight_imag[:, None, None, None] * green_all[:, 0], axis=0)
    density = jnp.sum(weight_real[:, None, None] * inverse_rows[:, 1] + weight_imag[:, None, None] * inverse_rows[:, 0], axis=0)
    owner_ids = row_owner[:, 0].reshape(NB, BLK)
    owner_hot = (owner_ids[:, :, None] == jnp.arange(N_POLE, dtype=jnp.int32)[None, None, :]).astype(jnp.int32)
    owner_rank = jnp.cumsum(owner_hot, axis=1) - owner_hot
    rank_own = jnp.sum(owner_hot * owner_rank, axis=2)
    slot_hit = (rank_own[:, :, None] == jnp.arange(CAP, dtype=jnp.int32)[None, None, :]).astype(jnp.float32)
    dens_blocks = density.reshape(NB, BLK, W)
    owned = jnp.einsum("btp,btc,btw->pbcw", owner_hot.astype(jnp.float32), slot_hit, dens_blocks, precision=lax.Precision.HIGHEST)
    owned_density = owned.reshape(N_POLE, NB * CAP, W)
    return inverse_rows, owned_density, block_density
```

```python
import functools

import jax
import jax.numpy as jnp
from jax import lax
from jax.experimental import pallas as pl
from jax.experimental.pallas import tpu as pltpu
from jax.sharding import PartitionSpec as P

MESH = pl.DeviceIdType.MESH
JOBS = ((0, 0), (1, 0), (0, 1), (1, 1))
NJ = len(JOBS)
F32, BF16 = jnp.float32, jnp.bfloat16


def split(value):
    high = value.astype(BF16)
    return high, (value - high.astype(F32)).astype(BF16)


def dot(left, right):
    return jnp.dot(left, right, preferred_element_type=F32)


def main_kernel(
    tiles_hbm, diag_hbm, factor, pattern, owner, anc, order, table,
    rows_out, dens_out, zed_out,
    tiles, diag, dens, zed, zcross, zpart, zplane, zline, chosen, picked, dgot, a_high, a_low, gath, l_high, l_low, prod, cross, sums, line, tile_sem, diag_sem,
    zs, zr, xs, xr, fs, fr, cs, cr, ls, lr,
    t0s, t0r, t1s, t1r, t2s, t2r, t3s, t3r, t4s, t4r, ds, dr,
):
    pole, row, col = lax.axis_index("pole"), lax.axis_index("row"), lax.axis_index("col")
    zl, core = row // 2, row % 2
    x, zh = col // 2, col % 2
    half = zl // 2
    inner = zl + half * (3 - 2 * zl)
    other_col = x * 2 + 1 - zh
    right_x, left_x = (x + 1) % 4, (x + 3) % 4

    partner = (pole, row, other_col)
    right = (pole, row, right_x * 2 + zh)
    left = (pole, row, left_x * 2 + zh)
    sibling = (pole, zl * 2 + 1 - core, col)
    mate = (pole, (1 - inner + half * (1 + 2 * inner)) * 2 + core, col)
    across = (pole, (3 - zl) * 2 + core, col)

    load = pltpu.make_async_copy(tiles_hbm, tiles, tile_sem)
    load.start()

    plane_at = pole * 4 + x
    z_at = zh * 4 + zl
    diag_load = pltpu.make_async_copy(
        diag_hbm.at[:, :, :, core * 16 + x * 4 + zl], diag, diag_sem
    )
    diag_load.start()

    def plane_peer(i):
        at = (plane_at + i) % 16
        return at, (at // 4, row, (at % 4) * 2 + zh)

    def line_peer(i):
        at = (z_at + i) % 8
        return (pole, (at % 4) * 2 + core, x * 2 + at // 4)

    barrier = pltpu.get_barrier_semaphore()

    def greet_plane(i, carry):
        pl.semaphore_signal(barrier, inc=1, device_id=plane_peer(i)[1], device_id_type=MESH)
        return carry

    def greet_line(i, carry):
        pl.semaphore_signal(barrier, inc=1, device_id=line_peer(i), device_id_type=MESH)
        return carry

    lax.fori_loop(1, 16, greet_plane, 0)
    lax.fori_loop(1, 8, greet_line, 0)
    pl.semaphore_signal(barrier, inc=1, device_id=sibling, device_id_type=MESH)

    block = row * 8 + col
    keeps = [anc[k, block].astype(F32) for k in range(2)]
    for j, (p, k) in enumerate(JOBS):
        gath[j, col] = factor[p, :, :, k * 256 : (k + 1) * 256] * keeps[k]

    pl.semaphore_wait(barrier, 23)

    def remote(src, dst, send, recv, peer):
        return pltpu.make_async_remote_copy(
            src_ref=src, dst_ref=dst, send_sem=send, recv_sem=recv, device_id=peer, device_id_type=MESH
        )

    def z_copy(j):
        return remote(gath.at[j, col], gath.at[j, col], zs.at[j], zr.at[j], partner)

    def z_recv(j):
        return remote(gath.at[j, other_col], gath.at[j, other_col], zs.at[j], zr.at[j], partner)

    def x_copy(j, h, d):
        slot = col if h == 0 else other_col
        peer = right if d == 0 else left
        return remote(gath.at[j, slot], gath.at[j, slot], xs.at[j, h, d], xr.at[j, h, d], peer)

    def x_slot(h, shift):
        half_of = zh if h == 0 else 1 - zh
        return ((x + shift) % 4) * 2 + half_of

    def x_recv(j, h, d):
        slot = x_slot(h, 3 if d == 0 else 1)
        return remote(gath.at[j, slot], gath.at[j, slot], xs.at[j, h, d], xr.at[j, h, d], right)

    def f_copy(j, h, d):
        slot = x_slot(h, 3 if d == 0 else 1)
        peer = right if d == 0 else left
        return remote(gath.at[j, slot, d], gath.at[j, slot, d], fs.at[j, h, d], fr.at[j, h, d], peer)

    def f_recv(j, h, d):
        slot = x_slot(h, 2)
        return remote(gath.at[j, slot, d], gath.at[j, slot, d], fs.at[j, h, d], fr.at[j, h, d], right)

    def z_forward(j):
        z_recv(j).wait_recv()
        for d in range(2):
            x_copy(j, 1, d).start()

    def x_forward(j, h):
        for d in range(2):
            x_recv(j, h, d).wait_recv()
            f_copy(j, h, d).start()

    def f_wait(j):
        for h in range(2):
            for d in range(2):
                f_recv(j, h, d).wait_recv()

    def prepare():
        load.wait()
        expand = (
            lax.broadcasted_iota(jnp.int32, (64, 512), 0)
            == row * 8 + lax.broadcasted_iota(jnp.int32, (64, 512), 1) // 64
        ).astype(BF16)
        tile_rows = jnp.concatenate(
            [pattern[pl.ds(g * 8 + col, 1), :] for g in range(8)], axis=0
        ).astype(F32).astype(BF16)
        keep_cols = dot(tile_rows, expand)
        for g in range(8):
            mask = keep_cols[g : g + 1, :]

            def one(i, carry, g=g, mask=mask):
                p, part = i // 2, i % 2
                high, low = split(tiles[p, part, g] * mask)
                a_high[p, part, g * 64 : (g + 1) * 64] = high
                a_low[p, part, g * 64 : (g + 1) * 64] = low
                return carry

            lax.fori_loop(0, 4, one, 0)

    def multiply(j):
        p, k = JOBS[j]

        def halves(c, carry):
            for part in range(2):
                high, low = split(gath[j, c, part])
                at = pl.ds(pl.multiple_of(c * 64, 64), 64)
                l_high[part, at] = high
                l_low[part, at] = low
                if part == 1:
                    l_high[2, at] = -high
                    l_low[2, at] = -low
            return carry

        lax.fori_loop(0, 8, halves, 0)

        def one(n, carry):
            total = None
            for part in range(2):
                pick = part * 2 * (1 - n) + (1 - part) * n
                bh, bl = l_high[pick], l_low[pick]
                ah, al = a_high[p, part], a_low[p, part]
                term = dot(ah, bh) + (dot(ah, bl) + dot(al, bh))
                total = term if total is None else total + term
            for g in range(8):
                prod[j, g, n] = total[g * 64 : (g + 1) * 64]
            return carry

        lax.fori_loop(0, 2, one, 0)
        for d in range(4):
            c_copy(j, d).start()

    def c_copy(j, d):
        return remote(prod.at[j, d * 2 + 1 - core], cross.at[j, d], cs.at[j, d], cr.at[j, d], sibling)

    def at_line(d):
        return d + half * (3 - 2 * d)

    def l_copy(j, slot, d, peer):
        return remote(sums.at[j, d], line.at[j, slot], ls.at[j, d], lr.at[j, slot], peer)

    def l_wait(j, slot):
        remote(sums.at[j, 0], line.at[j, slot], ls.at[j, 0], lr.at[j, slot], mate).wait_recv()

    def c_sum(j):
        for d in (3, 2, 1, 0):
            place = at_line(d)
            remote(prod.at[j, 0], cross.at[j, place], cs.at[j, d], cr.at[j, place], sibling).wait_recv()
            sums[j, d] = prod[j, place * 2 + core] + cross[j, place]
            if d > 0:

                @pl.when(inner == 0)
                def _(d=d):
                    l_copy(j, d - 1, d, mate).start()

    def l_mid(j):
        @pl.when(inner == 1)
        def _():
            for d in (3, 2):
                l_wait(j, d - 1)
                sums[j, d] = sums[j, d] + line[j, d - 1]
                l_copy(j, 6 - d, d, across).start()

    def l_end(j):
        @pl.when(inner == 1)
        def _():
            l_wait(j, 3)
            sums[j, 0] = sums[j, 0] + line[j, 3]
            l_copy(j, 3, 0, mate).start()
            l_wait(j, 0)
            l_wait(j, 4)
            sums[j, 1] = sums[j, 1] + (line[j, 0] + line[j, 4])

        @pl.when(inner == 0)
        def _():
            l_wait(j, 3)
            sums[j, 0] = sums[j, 0] + line[j, 3]

    def output(j):
        p, k = JOBS[j]
        at = slice(k * 256, (k + 1) * 256)
        done = sums[j, inner] * keeps[k]
        rows_out[p, :, :, at] = done
        entry = order[pole * 2 + p]
        wr, wi = table[entry, 0], table[entry, 1]
        fr_, fi_ = gath[j, col, 0], gath[j, col, 1]
        density = wr * done[1] + wi * done[0]
        left_side = jnp.concatenate([wr * fi_ + wi * fr_, wr * fr_ - wi * fi_], axis=0)
        right_side = jnp.concatenate([done[0], done[1]], axis=0)
        product = lax.dot_general(
            left_side, right_side, (((0,), (0,)), ((), ())),
            precision=lax.Precision.HIGHEST, preferred_element_type=F32,
        ).reshape(32, 8, 256)
        if p == 0:
            dens[k] = density
            zed[k] = -product
        else:
            dens[k] += density
            zed[k] -= product

    def choose():
        lanes = lax.broadcasted_iota(jnp.int32, (64, 128), 1)
        hot = (owner[...] == lanes // 32).astype(F32)
        before = (
            lax.broadcasted_iota(jnp.int32, (64, 64), 1) < lax.broadcasted_iota(jnp.int32, (64, 64), 0)
        ).astype(BF16)
        rank = dot(before, hot.astype(BF16))
        chosen[...] = jnp.where(rank == (lanes % 32).astype(F32), hot, 0.0)

    def d_copy(k, i):
        to = (pole + i) % 4
        return remote(picked.at[k, to], dgot.at[k, i - 1], ds.at[k], dr.at[k], (to, row, col))

    def d_send(k):
        picked[k] = lax.dot_general(
            chosen[...], dens[k], (((0,), (0,)), ((), ())),
            precision=lax.Precision.HIGHEST, preferred_element_type=F32,
        ).reshape(4, 32, 256)
        for i in range(1, 4):
            d_copy(k, i).start()

    def d_all(k):
        return remote(picked.at[k, 0:3], dgot.at[k], ds.at[k], dr.at[k], sibling)

    def d_take(k):
        d_all(k).wait_recv()
        dens_out[:, k * 256 : (k + 1) * 256] = picked[k, pole] + (dgot[k, 0] + dgot[k, 1] + dgot[k, 2])

    def t0_copy(k):
        return remote(zed.at[k, pl.ds((1 - core) * 16, 16)], zcross.at[k], t0s.at[k], t0r.at[k], sibling)

    def t1_send(k):
        t0_copy(k).wait_recv()
        zpart[k] = zed[k, pl.ds(core * 16, 16)] + zcross[k]

        @pl.when(zh == 0)
        def _():
            here = x * 4 + zl
            part = zpart[k, here]
            for p in range(2):
                entry = order[pole * 2 + p]
                part = part + (table[entry, 0] * diag[p, 1, k] + table[entry, 1] * diag[p, 0, k])
            zpart[k, here] = part

        def send(i, carry):
            at, peer = plane_peer(i)
            remote(zpart.at[k, at], zplane.at[k, i - 1], t1s.at[k], t1r.at[k], peer).start()
            return carry

        lax.fori_loop(1, 16, send, 0)

    def t1_all(k):
        return remote(zpart.at[k, 0:15], zplane.at[k], t1s.at[k], t1r.at[k], sibling)

    def t2_send(k):
        t1_all(k).wait_recv()
        zline[k, z_at] = zpart[k, plane_at] + jnp.sum(zplane[k], axis=0)

        def send(i, carry):
            here = zline.at[k, z_at]
            remote(here, here, t2s.at[k], t2r.at[k], line_peer(i)).start()
            return carry

        lax.fori_loop(1, 8, send, 0)

    def t2_all(k):
        return remote(zline.at[k, 0:7], zline.at[k, 0:7], t2s.at[k], t2r.at[k], sibling)

    def t3_send(k):
        t2_all(k).wait_recv()
        mine = zed_out.at[k, core * 16 + plane_at]
        mine[...] = jnp.sum(zline[k], axis=0)

        def send(i, carry):
            remote(mine, mine, t3s.at[k], t3r.at[k], plane_peer(i)[1]).start()
            return carry

        lax.fori_loop(1, 16, send, 0)

    def t3_all(k):
        here = zed_out.at[k, pl.ds(core * 16, 15)]
        return remote(here, here, t3s.at[k], t3r.at[k], sibling)

    def t4_copy(k):
        here = zed_out.at[k, pl.ds(core * 16, 16)]
        return remote(here, here, t4s.at[k], t4r.at[k], sibling)

    def t4_send(k):
        t3_all(k).wait_recv()
        t4_copy(k).start()

    def sum_start(k):
        t0_copy(k).start()
        d_send(k)

    for j in range(NJ):
        z_copy(j).start()
        for d in range(2):
            x_copy(j, 0, d).start()
    prepare()
    choose()
    diag_load.wait()
    x_forward(0, 0)
    z_forward(0)
    x_forward(1, 0)
    for j in range(NJ):
        x_forward(j, 1)
        if j + 1 < NJ:
            z_forward(j + 1)
        if j + 2 < NJ:
            x_forward(j + 2, 0)
        f_wait(j)
        multiply(j)
        if j >= 1:
            l_mid(j - 1)
        c_sum(j)
        if j >= 1:
            l_end(j - 1)
            output(j - 1)
        if j == 2:
            sum_start(0)
        if j == 3:
            t1_send(0)
    l_mid(NJ - 1)
    t2_send(0)
    l_end(NJ - 1)
    output(NJ - 1)
    sum_start(1)
    t3_send(0)
    t1_send(1)
    t4_send(0)
    t2_send(1)
    d_take(0)
    d_take(1)
    t3_send(1)
    t4_send(1)
    for k in range(2):
        t4_copy(k).wait_recv()

    for k in range(2):
        for copy in (t0_copy(k), t1_all(k), t2_all(k), t3_all(k), t4_copy(k), d_all(k)):
            copy.wait_send()
    for j in range(NJ):
        z_copy(j).wait_send()
        for h in range(2):
            for d in range(2):
                x_copy(j, h, d).wait_send()
                f_copy(j, h, d).wait_send()
        for d in range(4):
            c_copy(j, d).wait_send()

        @pl.when(inner == 0)
        def _(j=j):
            for d in (3, 2, 1):
                l_copy(j, d - 1, d, mate).wait_send()

        @pl.when(inner == 1)
        def _(j=j):
            for d in (3, 2, 0):
                l_copy(j, 0, d, mate).wait_send()


def main_call(tiles, diag, factor, pattern, owner, anc, order, table):
    vmem = pl.BlockSpec(memory_space=pltpu.VMEM)
    smem = pl.BlockSpec(memory_space=pltpu.SMEM)
    hbm = pl.BlockSpec(memory_space=pl.ANY)
    dma = pltpu.SemaphoreType.DMA
    return pl.pallas_call(
        main_kernel,
        out_shape=(
            jax.ShapeDtypeStruct((2, 2, 64, 512), F32),
            jax.ShapeDtypeStruct((32, 512), F32),
            jax.ShapeDtypeStruct((2, 32, 8, 256), F32),
        ),
        in_specs=[hbm, hbm, vmem, vmem, vmem, smem, smem, smem],
        out_specs=(vmem, vmem, vmem),
        scratch_shapes=[
            pltpu.VMEM((2, 2, 8, 64, 512), F32),
            pltpu.VMEM((2, 2, 2, 8, 256), F32),
            pltpu.VMEM((2, 64, 256), F32),
            pltpu.VMEM((2, 32, 8, 256), F32),
            pltpu.VMEM((2, 16, 8, 256), F32),
            pltpu.VMEM((2, 16, 8, 256), F32),
            pltpu.VMEM((2, 15, 8, 256), F32),
            pltpu.VMEM((2, 8, 8, 256), F32),
            pltpu.VMEM((64, 128), F32),
            pltpu.VMEM((2, 4, 32, 256), F32),
            pltpu.VMEM((2, 3, 32, 256), F32),
            pltpu.VMEM((2, 2, 512, 512), BF16),
            pltpu.VMEM((2, 2, 512, 512), BF16),
            pltpu.VMEM((NJ, 8, 2, 64, 256), F32),
            pltpu.VMEM((3, 512, 256), BF16),
            pltpu.VMEM((3, 512, 256), BF16),
            pltpu.VMEM((NJ, 8, 2, 64, 256), F32),
            pltpu.VMEM((NJ, 4, 2, 64, 256), F32),
            pltpu.VMEM((NJ, 4, 2, 64, 256), F32),
            pltpu.VMEM((NJ, 5, 2, 64, 256), F32),
            dma, dma,
            dma((NJ,)), dma((NJ,)),
            dma((NJ, 2, 2)), dma((NJ, 2, 2)),
            dma((NJ, 2, 2)), dma((NJ, 2, 2)),
            dma((NJ, 4)), dma((NJ, 4)),
            dma((NJ, 4)), dma((NJ, 5)),
            *([dma((2,))] * 12),
        ],
        compiler_params=pltpu.CompilerParams(
            collective_id=0, has_side_effects=True, vmem_limit_bytes=60 * 2**20
        ),
    )(tiles, diag, factor, pattern, owner, anc, order, table)


def shards(tiles, factor, diag, pattern, anc, row_owner, table, order):
    rows, dens, zed = main_call(
        tiles, diag.reshape(2, 2, 2, 32, 8, 256), factor, pattern, row_owner, anc, order, table
    )
    return rows, dens[None], zed.reshape(2, 256, 256)


def solution(mesh):
    placed = (
        P("pole", None, None, "col", "row"),
        P("pole", None, ("row", "col"), None),
        P("pole", None, None, None, None),
        P(),
        P(),
        P(("row", "col"), None),
        P(),
        P(),
    )
    return jax.shard_map(
        shards,
        mesh=mesh,
        in_specs=placed,
        out_specs=(P("pole", None, ("row", "col"), None), P("pole", ("row", "col"), None), P()),
        check_vma=False,
    )
```

```python
import functools

import jax
import jax.numpy as jnp
from jax import lax
from jax.experimental import pallas as pl
from jax.experimental.pallas import tpu as pltpu
from jax.sharding import PartitionSpec as P

MESH = pl.DeviceIdType.MESH
JOBS = ((0, 0), (1, 0), (0, 1), (1, 1))
NJ = len(JOBS)
F32, BF16 = jnp.float32, jnp.bfloat16


def split(value):
    high = value.astype(BF16)
    return high, (value - high.astype(F32)).astype(BF16)


def dot(left, right):
    return jnp.dot(left, right, preferred_element_type=F32)


def main_kernel(
    tiles_hbm, diag_hbm, factor, pattern, owner, anc, order, table,
    rows_out, dens_out, zed_out,
    tiles, diag, dens, zed, zcross, zpart, zplane, zline, chosen, picked, dgot, a_high, a_low, gath, l_high, l_low, prod, cross, sums, line, tile_sem, diag_sem,
    zs, zr, xs, xr, fs, fr, cs, cr, ls, lr,
    t0s, t0r, t1s, t1r, t2s, t2r, t3s, t3r, t4s, t4r, ds, dr,
):
    pole, row, col = lax.axis_index("pole"), lax.axis_index("row"), lax.axis_index("col")
    zl, core = row // 2, row % 2
    x, zh = col // 2, col % 2
    half = zl // 2
    inner = zl + half * (3 - 2 * zl)
    other_col = x * 2 + 1 - zh
    right_x, left_x = (x + 1) % 4, (x + 3) % 4

    partner = (pole, row, other_col)
    right = (pole, row, right_x * 2 + zh)
    left = (pole, row, left_x * 2 + zh)
    sibling = (pole, zl * 2 + 1 - core, col)
    mate = (pole, (1 - inner + half * (1 + 2 * inner)) * 2 + core, col)
    across = (pole, (3 - zl) * 2 + core, col)

    load = pltpu.make_async_copy(tiles_hbm, tiles, tile_sem)
    load.start()

    plane_at = pole * 4 + x
    z_at = zh * 4 + zl
    diag_load = pltpu.make_async_copy(
        diag_hbm.at[:, :, :, core * 16 + x * 4 + zl], diag, diag_sem
    )
    diag_load.start()

    def plane_peer(i):
        at = (plane_at + i) % 16
        return at, (at // 4, row, (at % 4) * 2 + zh)

    def line_peer(i):
        at = (z_at + i) % 8
        return (pole, (at % 4) * 2 + core, x * 2 + at // 4)

    barrier = pltpu.get_barrier_semaphore()

    def greet_plane(i, carry):
        pl.semaphore_signal(barrier, inc=1, device_id=plane_peer(i)[1], device_id_type=MESH)
        return carry

    def greet_line(i, carry):
        pl.semaphore_signal(barrier, inc=1, device_id=line_peer(i), device_id_type=MESH)
        return carry

    lax.fori_loop(1, 16, greet_plane, 0)
    lax.fori_loop(1, 8, greet_line, 0)
    pl.semaphore_signal(barrier, inc=1, device_id=sibling, device_id_type=MESH)

    block = row * 8 + col
    keeps = [anc[k, block].astype(F32) for k in range(2)]
    for j, (p, k) in enumerate(JOBS):
        gath[j, col] = factor[p, :, :, k * 256 : (k + 1) * 256] * keeps[k]

    pl.semaphore_wait(barrier, 23)

    def remote(src, dst, send, recv, peer):
        return pltpu.make_async_remote_copy(
            src_ref=src, dst_ref=dst, send_sem=send, recv_sem=recv, device_id=peer, device_id_type=MESH
        )

    def z_copy(j):
        return remote(gath.at[j, col], gath.at[j, col], zs.at[j], zr.at[j], partner)

    def z_recv(j):
        return remote(gath.at[j, other_col], gath.at[j, other_col], zs.at[j], zr.at[j], partner)

    def x_copy(j, h, d):
        slot = col if h == 0 else other_col
        peer = right if d == 0 else left
        return remote(gath.at[j, slot], gath.at[j, slot], xs.at[j, h, d], xr.at[j, h, d], peer)

    def x_slot(h, shift):
        half_of = zh if h == 0 else 1 - zh
        return ((x + shift) % 4) * 2 + half_of

    def x_recv(j, h, d):
        slot = x_slot(h, 3 if d == 0 else 1)
        return remote(gath.at[j, slot], gath.at[j, slot], xs.at[j, h, d], xr.at[j, h, d], right)

    def f_copy(j, h, d):
        slot = x_slot(h, 3 if d == 0 else 1)
        peer = right if d == 0 else left
        return remote(gath.at[j, slot, d], gath.at[j, slot, d], fs.at[j, h, d], fr.at[j, h, d], peer)

    def f_recv(j, h, d):
        slot = x_slot(h, 2)
        return remote(gath.at[j, slot, d], gath.at[j, slot, d], fs.at[j, h, d], fr.at[j, h, d], right)

    def z_forward(j):
        z_recv(j).wait_recv()
        for d in range(2):
            x_copy(j, 1, d).start()

    def x_forward(j, h):
        for d in range(2):
            x_recv(j, h, d).wait_recv()
            f_copy(j, h, d).start()

    def f_wait(j):
        for h in range(2):
            for d in range(2):
                f_recv(j, h, d).wait_recv()

    def prepare():
        load.wait()
        expand = (
            lax.broadcasted_iota(jnp.int32, (64, 512), 0)
            == row * 8 + lax.broadcasted_iota(jnp.int32, (64, 512), 1) // 64
        ).astype(BF16)
        tile_rows = jnp.concatenate(
            [pattern[pl.ds(g * 8 + col, 1), :] for g in range(8)], axis=0
        ).astype(F32).astype(BF16)
        keep_cols = dot(tile_rows, expand)
        for g in range(8):
            mask = keep_cols[g : g + 1, :]

            def one(i, carry, g=g, mask=mask):
                p, part = i // 2, i % 2
                high, low = split(tiles[p, part, g] * mask)
                a_high[p, part, g * 64 : (g + 1) * 64] = high
                a_low[p, part, g * 64 : (g + 1) * 64] = low
                return carry

            lax.fori_loop(0, 4, one, 0)

    def multiply(j):
        p, k = JOBS[j]

        def halves(c, carry):
            for part in range(2):
                high, low = split(gath[j, c, part])
                at = pl.ds(pl.multiple_of(c * 64, 64), 64)
                l_high[part, at] = high
                l_low[part, at] = low
                if part == 1:
                    l_high[2, at] = -high
                    l_low[2, at] = -low
            return carry

        lax.fori_loop(0, 8, halves, 0)

        def one(n, carry):
            total = None
            for part in range(2):
                pick = part * 2 * (1 - n) + (1 - part) * n
                bh, bl = l_high[pick], l_low[pick]
                ah, al = a_high[p, part], a_low[p, part]
                term = dot(ah, bh) + (dot(ah, bl) + dot(al, bh))
                total = term if total is None else total + term
            for g in range(8):
                prod[j, g, n] = total[g * 64 : (g + 1) * 64]
            return carry

        lax.fori_loop(0, 2, one, 0)
        for d in range(4):
            c_copy(j, d).start()

    def c_copy(j, d):
        return remote(prod.at[j, d * 2 + 1 - core], cross.at[j, d], cs.at[j, d], cr.at[j, d], sibling)

    def at_line(d):
        return d + half * (3 - 2 * d)

    def l_copy(j, slot, d, peer):
        return remote(sums.at[j, d], line.at[j, slot], ls.at[j, d], lr.at[j, slot], peer)

    def l_wait(j, slot):
        remote(sums.at[j, 0], line.at[j, slot], ls.at[j, 0], lr.at[j, slot], mate).wait_recv()

    def c_sum(j):
        for d in (3, 2, 1, 0):
            place = at_line(d)
            remote(prod.at[j, 0], cross.at[j, place], cs.at[j, d], cr.at[j, place], sibling).wait_recv()
            sums[j, d] = prod[j, place * 2 + core] + cross[j, place]
            if d > 0:

                @pl.when(inner == 0)
                def _(d=d):
                    l_copy(j, d - 1, d, mate).start()

    def l_mid(j):
        @pl.when(inner == 1)
        def _():
            for d in (3, 2):
                l_wait(j, d - 1)
                sums[j, d] = sums[j, d] + line[j, d - 1]
                l_copy(j, 6 - d, d, across).start()

    def l_end(j):
        @pl.when(inner == 1)
        def _():
            l_wait(j, 3)
            sums[j, 0] = sums[j, 0] + line[j, 3]
            l_copy(j, 3, 0, mate).start()
            l_wait(j, 0)
            l_wait(j, 4)
            sums[j, 1] = sums[j, 1] + (line[j, 0] + line[j, 4])

        @pl.when(inner == 0)
        def _():
            l_wait(j, 3)
            sums[j, 0] = sums[j, 0] + line[j, 3]

    def output(j):
        p, k = JOBS[j]
        at = slice(k * 256, (k + 1) * 256)
        done = sums[j, inner] * keeps[k]
        rows_out[p, :, :, at] = done
        entry = order[pole * 2 + p]
        wr, wi = table[0, entry], table[1, entry]
        fr_, fi_ = gath[j, col, 0], gath[j, col, 1]
        density = wr * done[1] + wi * done[0]
        left_side = jnp.concatenate([wr * fi_ + wi * fr_, wr * fr_ - wi * fi_], axis=0)
        right_side = jnp.concatenate([done[0], done[1]], axis=0)
        product = lax.dot_general(
            left_side, right_side, (((0,), (0,)), ((), ())),
            precision=lax.Precision.HIGHEST, preferred_element_type=F32,
        ).reshape(32, 8, 256)
        if p == 0:
            dens[k] = density
            zed[k] = -product
        else:
            dens[k] += density
            zed[k] -= product

    def choose():
        lines = lax.broadcasted_iota(jnp.int32, (128, 64), 0)
        hot = (owner[...] == lines // 32).astype(F32)
        before = (
            lax.broadcasted_iota(jnp.int32, (64, 64), 0) < lax.broadcasted_iota(jnp.int32, (64, 64), 1)
        ).astype(BF16)
        rank = dot(hot.astype(BF16), before)
        chosen[...] = jnp.where(rank == (lines % 32).astype(F32), hot, 0.0)

    def d_copy(k, i):
        to = (pole + i) % 4
        return remote(picked.at[k, to], dgot.at[k, i - 1], ds.at[k], dr.at[k], (to, row, col))

    def d_send(k):
        picked[k] = lax.dot_general(
            chosen[...], dens[k], (((1,), (0,)), ((), ())),
            precision=lax.Precision.HIGHEST, preferred_element_type=F32,
        ).reshape(4, 32, 256)
        for i in range(1, 4):
            d_copy(k, i).start()

    def d_all(k):
        return remote(picked.at[k, 0:3], dgot.at[k], ds.at[k], dr.at[k], sibling)

    def d_take(k):
        d_all(k).wait_recv()
        dens_out[:, k * 256 : (k + 1) * 256] = picked[k, pole] + (dgot[k, 0] + dgot[k, 1] + dgot[k, 2])

    def t0_copy(k):
        return remote(zed.at[k, pl.ds((1 - core) * 16, 16)], zcross.at[k], t0s.at[k], t0r.at[k], sibling)

    def t1_send(k):
        t0_copy(k).wait_recv()
        zpart[k] = zed[k, pl.ds(core * 16, 16)] + zcross[k]

        @pl.when(zh == 0)
        def _():
            here = x * 4 + zl
            part = zpart[k, here]
            for p in range(2):
                entry = order[pole * 2 + p]
                part = part + (table[0, entry] * diag[p, 1, k] + table[1, entry] * diag[p, 0, k])
            zpart[k, here] = part

        def send(i, carry):
            at, peer = plane_peer(i)
            remote(zpart.at[k, at], zplane.at[k, i - 1], t1s.at[k], t1r.at[k], peer).start()
            return carry

        lax.fori_loop(1, 16, send, 0)

    def t1_all(k):
        return remote(zpart.at[k, 0:15], zplane.at[k], t1s.at[k], t1r.at[k], sibling)

    def t2_send(k):
        t1_all(k).wait_recv()
        zline[k, z_at] = zpart[k, plane_at] + jnp.sum(zplane[k], axis=0)

        def send(i, carry):
            here = zline.at[k, z_at]
            remote(here, here, t2s.at[k], t2r.at[k], line_peer(i)).start()
            return carry

        lax.fori_loop(1, 8, send, 0)

    def t2_all(k):
        return remote(zline.at[k, 0:7], zline.at[k, 0:7], t2s.at[k], t2r.at[k], sibling)

    def t3_send(k):
        t2_all(k).wait_recv()
        mine = zed_out.at[k, core * 16 + plane_at]
        mine[...] = jnp.sum(zline[k], axis=0)

        def send(i, carry):
            remote(mine, mine, t3s.at[k], t3r.at[k], plane_peer(i)[1]).start()
            return carry

        lax.fori_loop(1, 16, send, 0)

    def t3_all(k):
        here = zed_out.at[k, pl.ds(core * 16, 15)]
        return remote(here, here, t3s.at[k], t3r.at[k], sibling)

    def t4_copy(k):
        here = zed_out.at[k, pl.ds(core * 16, 16)]
        return remote(here, here, t4s.at[k], t4r.at[k], sibling)

    def t4_send(k):
        t3_all(k).wait_recv()
        t4_copy(k).start()

    def sum_start(k):
        t0_copy(k).start()
        d_send(k)

    def own_start(j):
        for d in range(2):
            x_copy(j, 0, d).start()

    def z_next(j):
        z_copy(j - 1).wait_send()
        z_copy(j).start()

    z_copy(0).start()
    own_start(0)
    own_start(1)
    prepare()
    z_next(1)
    x_forward(0, 0)
    own_start(2)
    choose()
    diag_load.wait()
    z_forward(0)
    z_next(2)
    x_forward(1, 0)
    x_forward(0, 1)
    own_start(3)
    z_forward(1)
    z_next(3)
    x_forward(2, 0)
    f_wait(0)
    multiply(0)
    x_forward(1, 1)
    c_sum(0)
    z_forward(2)
    x_forward(3, 0)
    f_wait(1)
    multiply(1)
    x_forward(2, 1)
    z_forward(3)
    l_mid(0)
    c_sum(1)
    f_wait(2)
    multiply(2)
    x_forward(3, 1)
    l_end(0)
    output(0)
    l_mid(1)
    c_sum(2)
    f_wait(3)
    multiply(3)
    l_end(1)
    output(1)
    sum_start(0)
    c_sum(3)
    l_mid(2)
    t1_send(0)
    l_end(2)
    output(2)
    t2_send(0)
    l_mid(3)
    t3_send(0)
    l_end(3)
    output(3)
    sum_start(1)
    t1_send(1)
    t4_send(0)
    t2_send(1)
    d_take(0)
    d_take(1)
    t3_send(1)
    t4_send(1)
    for k in range(2):
        t4_copy(k).wait_recv()

    for k in range(2):
        for copy in (t0_copy(k), t1_all(k), t2_all(k), t3_all(k), t4_copy(k), d_all(k)):
            copy.wait_send()
    for j in range(NJ):
        if j == NJ - 1:
            z_copy(j).wait_send()
        for h in range(2):
            for d in range(2):
                x_copy(j, h, d).wait_send()
                f_copy(j, h, d).wait_send()
        for d in range(4):
            c_copy(j, d).wait_send()

        @pl.when(inner == 0)
        def _(j=j):
            for d in (3, 2, 1):
                l_copy(j, d - 1, d, mate).wait_send()

        @pl.when(inner == 1)
        def _(j=j):
            for d in (3, 2, 0):
                l_copy(j, 0, d, mate).wait_send()


def main_call(tiles, diag, factor, pattern, owner, anc, order, table):
    vmem = pl.BlockSpec(memory_space=pltpu.VMEM)
    smem = pl.BlockSpec(memory_space=pltpu.SMEM)
    hbm = pl.BlockSpec(memory_space=pl.ANY)
    dma = pltpu.SemaphoreType.DMA
    return pl.pallas_call(
        main_kernel,
        out_shape=(
            jax.ShapeDtypeStruct((2, 2, 64, 512), F32),
            jax.ShapeDtypeStruct((32, 512), F32),
            jax.ShapeDtypeStruct((2, 32, 8, 256), F32),
        ),
        in_specs=[hbm, hbm, vmem, vmem, vmem, smem, smem, smem],
        out_specs=(vmem, vmem, vmem),
        scratch_shapes=[
            pltpu.VMEM((2, 2, 8, 64, 512), F32),
            pltpu.VMEM((2, 2, 2, 8, 256), F32),
            pltpu.VMEM((2, 64, 256), F32),
            pltpu.VMEM((2, 32, 8, 256), F32),
            pltpu.VMEM((2, 16, 8, 256), F32),
            pltpu.VMEM((2, 16, 8, 256), F32),
            pltpu.VMEM((2, 15, 8, 256), F32),
            pltpu.VMEM((2, 8, 8, 256), F32),
            pltpu.VMEM((128, 64), F32),
            pltpu.VMEM((2, 4, 32, 256), F32),
            pltpu.VMEM((2, 3, 32, 256), F32),
            pltpu.VMEM((2, 2, 512, 512), BF16),
            pltpu.VMEM((2, 2, 512, 512), BF16),
            pltpu.VMEM((NJ, 8, 2, 64, 256), F32),
            pltpu.VMEM((3, 512, 256), BF16),
            pltpu.VMEM((3, 512, 256), BF16),
            pltpu.VMEM((NJ, 8, 2, 64, 256), F32),
            pltpu.VMEM((NJ, 4, 2, 64, 256), F32),
            pltpu.VMEM((NJ, 4, 2, 64, 256), F32),
            pltpu.VMEM((NJ, 5, 2, 64, 256), F32),
            dma, dma,
            dma((NJ,)), dma((NJ,)),
            dma((NJ, 2, 2)), dma((NJ, 2, 2)),
            dma((NJ, 2, 2)), dma((NJ, 2, 2)),
            dma((NJ, 4)), dma((NJ, 4)),
            dma((NJ, 4)), dma((NJ, 5)),
            *([dma((2,))] * 12),
        ],
        compiler_params=pltpu.CompilerParams(
            collective_id=0, has_side_effects=True, vmem_limit_bytes=60 * 2**20
        ),
    )(tiles, diag, factor, pattern, owner, anc, order, table)


def finish_kernel(rows, dens, zed, rows_out, dens_out, zed_out):
    rows_out[...] = rows[...]
    dens_out[...] = dens[...]
    zed_out[...] = zed[...]


def finish_call(rows, dens, zed):
    vmem = pl.BlockSpec(memory_space=pltpu.VMEM)
    return pl.pallas_call(
        finish_kernel,
        out_shape=tuple(jax.ShapeDtypeStruct(v.shape, v.dtype) for v in (rows, dens, zed)),
        in_specs=[vmem] * 3,
        out_specs=(vmem,) * 3,
    )(rows, dens, zed)


def shards(tiles, factor, diag, pattern, anc, row_owner, table, order):
    rows, dens, zed = main_call(
        tiles,
        diag.reshape(2, 2, 2, 32, 8, 256),
        factor,
        pattern,
        row_owner.reshape(1, 64),
        anc,
        order,
        table.T,
    )
    rows, dens, zed = finish_call(rows, dens, zed)
    return rows, dens[None], zed.reshape(2, 256, 256)


def solution(mesh):
    placed = (
        P("pole", None, None, "col", "row"),
        P("pole", None, ("row", "col"), None),
        P("pole", None, None, None, None),
        P(),
        P(),
        P(("row", "col"), None),
        P(),
        P(),
    )
    return jax.shard_map(
        shards,
        mesh=mesh,
        in_specs=placed,
        out_specs=(P("pole", None, ("row", "col"), None), P("pole", ("row", "col"), None), P()),
        check_vma=False,
    )
```

```python
import functools

import jax
import jax.numpy as jnp
from jax import lax
from jax.experimental import pallas as pl
from jax.experimental.pallas import tpu as pltpu
from jax.sharding import PartitionSpec as P

MESH = pl.DeviceIdType.MESH
JOBS = ((0, 0, 0, 2), (1, 0, 0, 2), (0, 1, 0, 2), (1, 1, 0, 2))
NJ = len(JOBS)
EARLY = 1
F32, BF16 = jnp.float32, jnp.bfloat16


def split(value):
    high = value.astype(BF16)
    return high, (value - high.astype(F32)).astype(BF16)


def dot(left, right):
    return jnp.dot(left, right, preferred_element_type=F32)


def main_kernel(
    tiles_hbm, diag_hbm, factor, pattern, owner, anc, order, table,
    rows_out, dens_out, zed_out,
    tiles, diag, dens, zed, zcross, zpart, zplane, zline, chosen, picked, dgot, peers_l, a_high, a_low, gath, l_high, l_low, prod, cross, sums, line, tile_sem, diag_sem,
    zs, zr, xs, xr, fs, fr, cs, cr, ls, lr,
    gs, gr, t0s, t0r, t1s, t1r, t2s, t2r, t3s, t3r, t4s, t4r, ds, dr,
):
    pole, row, col = lax.axis_index("pole"), lax.axis_index("row"), lax.axis_index("col")
    zl, core = row // 2, row % 2
    x, zh = col // 2, col % 2
    half = zl // 2
    inner = zl + half * (3 - 2 * zl)
    other_col = x * 2 + 1 - zh
    right_x, left_x = (x + 1) % 4, (x + 3) % 4

    partner = (pole, row, other_col)
    right = (pole, row, right_x * 2 + zh)
    left = (pole, row, left_x * 2 + zh)
    sibling = (pole, zl * 2 + 1 - core, col)
    mate = (pole, (1 - inner + half * (1 + 2 * inner)) * 2 + core, col)
    across = (pole, (3 - zl) * 2 + core, col)

    load = pltpu.make_async_copy(tiles_hbm, tiles, tile_sem)
    load.start()

    plane_at = pole * 4 + x
    z_at = zh * 4 + zl
    diag_load = pltpu.make_async_copy(
        diag_hbm.at[:, :, :, core * 16 + x * 4 + zl], diag, diag_sem
    )
    diag_load.start()

    def plane_peer(i):
        at = (plane_at + i) % 16
        return at, (at // 4, row, (at % 4) * 2 + zh)

    def line_peer(i):
        at = (z_at + i) % 8
        return (pole, (at % 4) * 2 + core, x * 2 + at // 4)

    barrier = pltpu.get_barrier_semaphore()

    def greet_plane(i, carry):
        pl.semaphore_signal(barrier, inc=1, device_id=plane_peer(i)[1], device_id_type=MESH)
        return carry

    def greet_line(i, carry):
        pl.semaphore_signal(barrier, inc=1, device_id=line_peer(i), device_id_type=MESH)
        return carry

    lax.fori_loop(1, 16, greet_plane, 0)
    lax.fori_loop(1, 8, greet_line, 0)
    pl.semaphore_signal(barrier, inc=1, device_id=sibling, device_id_type=MESH)

    block = row * 8 + col
    keeps = [anc[k, block].astype(F32) for k in range(2)]
    zed[...] = jnp.zeros_like(zed)
    for p in range(2):
        for k in range(2):
            for h in range(2):
                first = k * 256 + h * 128
                gath[k * 2 + p, col, h] = factor[p, :, :, first : first + 128] * keeps[k]

    pl.semaphore_wait(barrier, 23)

    def remote(src, dst, send, recv, peer):
        return pltpu.make_async_remote_copy(
            src_ref=src, dst_ref=dst, send_sem=send, recv_sem=recv, device_id=peer, device_id_type=MESH
        )

    def view(ref, j, *at):
        p, k, first, count = JOBS[j]
        return ref.at[(k * 2 + p, *at, pl.ds(first, count))]

    def half_view(j, slot, d):
        p, k, first, count = JOBS[j]
        return gath.at[k * 2 + p, slot, d] if count == 2 else gath.at[k * 2 + p, slot, first, d]

    def z_copy(j):
        return remote(view(gath, j, col), view(gath, j, col), zs.at[j], zr.at[j], partner)

    def z_recv(j):
        return remote(view(gath, j, other_col), view(gath, j, other_col), zs.at[j], zr.at[j], partner)

    def x_copy(j, h, d):
        slot = col if h == 0 else other_col
        peer = right if d == 0 else left
        return remote(view(gath, j, slot), view(gath, j, slot), xs.at[j, h, d], xr.at[j, h, d], peer)

    def x_slot(h, shift):
        half_of = zh if h == 0 else 1 - zh
        return ((x + shift) % 4) * 2 + half_of

    def x_recv(j, h, d):
        slot = x_slot(h, 3 if d == 0 else 1)
        return remote(view(gath, j, slot), view(gath, j, slot), xs.at[j, h, d], xr.at[j, h, d], right)

    def f_copy(j, h, d):
        slot = x_slot(h, 3 if d == 0 else 1)
        peer = right if d == 0 else left
        return remote(half_view(j, slot, d), half_view(j, slot, d), fs.at[j, h, d], fr.at[j, h, d], peer)

    def f_recv(j, h, d):
        slot = x_slot(h, 2)
        return remote(half_view(j, slot, d), half_view(j, slot, d), fs.at[j, h, d], fr.at[j, h, d], right)

    def z_forward(j):
        z_recv(j).wait_recv()
        for d in range(2):
            x_copy(j, 1, d).start()

    def x_forward(j, h):
        for d in range(2):
            x_recv(j, h, d).wait_recv()
            f_copy(j, h, d).start()

    def f_wait(j):
        for h in range(2):
            for d in range(2):
                f_recv(j, h, d).wait_recv()

    def prepare():
        load.wait()
        expand = (
            lax.broadcasted_iota(jnp.int32, (64, 512), 0)
            == row * 8 + lax.broadcasted_iota(jnp.int32, (64, 512), 1) // 64
        ).astype(BF16)
        tile_rows = jnp.concatenate(
            [pattern[pl.ds(g * 8 + col, 1), :] for g in range(8)], axis=0
        ).astype(F32).astype(BF16)
        keep_cols = dot(tile_rows, expand)
        for g in range(8):
            mask = keep_cols[g : g + 1, :]

            def one(i, carry, g=g, mask=mask):
                p, part = i // 2, i % 2
                high, low = split(tiles[p, part, g] * mask)
                a_high[p, part, g * 64 : (g + 1) * 64] = high
                a_low[p, part, g * 64 : (g + 1) * 64] = low
                return carry

            lax.fori_loop(0, 4, one, 0)

    def multiply(j):
        p, k, first, count = JOBS[j]
        b = k * 2 + p

        def halves(c, carry):
            at = pl.ds(pl.multiple_of(c * 64, 64), 64)
            for h in range(first, first + count):
                for part in range(2):
                    high, low = split(gath[b, c, h, part])
                    same = slice(h * 256 + part * 128, h * 256 + part * 128 + 128)
                    turned = slice(h * 256 + 128 - part * 128, h * 256 + 256 - part * 128)
                    l_high[0, at, same] = high
                    l_low[0, at, same] = low
                    l_high[1, at, turned] = -high if part else high
                    l_low[1, at, turned] = -low if part else low
            return carry

        lax.fori_loop(0, 8, halves, 0)

        def one(h, carry):
            at = pl.ds(pl.multiple_of(h * 256, 256), 256)
            total = None
            for part in range(2):
                bh, bl = l_high[part, :, at], l_low[part, :, at]
                ah, al = a_high[p, part], a_low[p, part]
                term = dot(ah, bh) + (dot(ah, bl) + dot(al, bh))
                total = term if total is None else total + term
            for g in range(8):
                rows = total[g * 64 : (g + 1) * 64]
                prod[b, g, h, 0] = rows[:, :128]
                prod[b, g, h, 1] = rows[:, 128:]
            return carry

        lax.fori_loop(first, first + count, one, 0)
        for d in range(4):
            c_copy(j, d).start()

    def c_copy(j, d):
        return remote(
            view(prod, j, d * 2 + 1 - core), view(cross, j, d), cs.at[j, d], cr.at[j, d], sibling
        )

    def at_line(d):
        return d + half * (3 - 2 * d)

    def l_copy(j, slot, d, peer):
        return remote(view(sums, j, d), view(line, j, slot), ls.at[j, d], lr.at[j, slot], peer)

    def l_wait(j, slot):
        l_copy(j, slot, 0, mate).wait_recv()
        return view(line, j, slot)[...]

    def c_sum(j):
        for d in (3, 2, 1, 0):
            place = at_line(d)
            remote(
                view(prod, j, 0), view(cross, j, place), cs.at[j, d], cr.at[j, place], sibling
            ).wait_recv()
            view(sums, j, d)[...] = view(prod, j, place * 2 + core)[...] + view(cross, j, place)[...]
            if d > 0:

                @pl.when(inner == 0)
                def _(d=d):
                    l_copy(j, d - 1, d, mate).start()

    def l_mid(j):
        @pl.when(inner == 1)
        def _():
            for d in (3, 2):
                here = view(sums, j, d)
                here[...] = here[...] + l_wait(j, d - 1)
                l_copy(j, 6 - d, d, across).start()

    def l_end(j):
        @pl.when(inner == 1)
        def _():
            here = view(sums, j, 0)
            here[...] = here[...] + l_wait(j, 3)
            l_copy(j, 3, 0, mate).start()
            here = view(sums, j, 1)
            here[...] = here[...] + (l_wait(j, 0) + l_wait(j, 4))

        @pl.when(inner == 0)
        def _():
            here = view(sums, j, 0)
            here[...] = here[...] + l_wait(j, 3)

    def output(j):
        p, k, first, count = JOBS[j]
        entry = order[pole * 2 + p]
        wr, wi = table[0, entry], table[1, entry]
        done = view(sums, j, inner)[...] * keeps[k]
        for i in range(count):
            lanes = slice((first + i) * 128, (first + i + 1) * 128)
            rows_out[p, :, :, k * 256 + lanes.start : k * 256 + lanes.stop] = done[i]
            density = wr * done[i, 1] + wi * done[i, 0]
            if p == 0:
                dens[k, :, lanes] = density
            else:
                dens[k, :, lanes] += density
        if k != EARLY:
            zed_add(j, weighted(gath[k * 2 + p, col], p), done)

    def weighted(block, p):
        entry = order[pole * 2 + p]
        wr, wi = table[0, entry], table[1, entry]
        panels = [
            jnp.concatenate(
                [wr * block[h, 1] + wi * block[h, 0], wr * block[h, 0] - wi * block[h, 1]], axis=0
            )
            for h in range(2)
        ]
        return jnp.concatenate(panels, axis=1)

    def zed_add(j, left_side, values):
        p, k, first, count = JOBS[j]
        for i in range(count):
            product = lax.dot_general(
                left_side, values[i].reshape(128, 128), (((0,), (0,)), ((), ())),
                precision=lax.Precision.HIGHEST, preferred_element_type=F32,
            ).reshape(32, 8, 128)
            zed[k, :, :, (first + i) * 128 : (first + i + 1) * 128] -= product

    def g_copy(p, source, place, at, peer):
        return remote(source, peers_l.at[p, place], gs.at[p, at], gr.at[p, place], peer)

    def g_own(p, at, peer):
        return g_copy(p, gath.at[2 + p, col], zl, at, peer)

    def g_wait(p, d):
        g_copy(p, gath.at[2 + p, col], at_line(d), 0, mate).wait_recv()

    def g_pass(p, d, at, peer):
        place = at_line(d)
        return g_copy(p, peers_l.at[p, place], place, at, peer)

    def g_start(p):
        peers_l[p, zl] = gath[2 + p, col]

        @pl.when(inner == 0)
        def _():
            g_own(p, 0, mate).start()

        @pl.when(inner == 1)
        def _():
            g_own(p, 0, across).start()
            g_own(p, 1, mate).start()

    def g_mid(p):
        @pl.when(inner == 1)
        def _():
            g_wait(p, 0)
            g_pass(p, 0, 2, across).start()
            g_wait(p, 2)
            g_pass(p, 2, 3, mate).start()

    def g_far(p):
        @pl.when(inner == 1)
        def _():
            g_wait(p, 3)
            g_pass(p, 3, 4, mate).start()

    def g_end(p):
        @pl.when(inner == 0)
        def _():
            for d in (1, 2, 3):
                g_wait(p, d)

    def zed_early(j):
        p = JOBS[j][0]

        def one(d, carry):
            zed_add(j, weighted(peers_l[p, at_line(d)], p), view(sums, j, d)[...])
            return carry

        lax.fori_loop(0, 4, one, 0)

    def choose():
        lines = lax.broadcasted_iota(jnp.int32, (128, 64), 0)
        hot = (owner[...] == lines // 32).astype(F32)
        before = (
            lax.broadcasted_iota(jnp.int32, (64, 64), 0) < lax.broadcasted_iota(jnp.int32, (64, 64), 1)
        ).astype(BF16)
        rank = dot(hot.astype(BF16), before)
        chosen[...] = jnp.where(rank == (lines % 32).astype(F32), hot, 0.0)

    def d_copy(k, i):
        to = (pole + i) % 4
        return remote(picked.at[k, to], dgot.at[k, i - 1], ds.at[k], dr.at[k], (to, row, col))

    def d_send(k):
        picked[k] = lax.dot_general(
            chosen[...], dens[k], (((1,), (0,)), ((), ())),
            precision=lax.Precision.HIGHEST, preferred_element_type=F32,
        ).reshape(4, 32, 256)
        for i in range(1, 4):
            d_copy(k, i).start()

    def d_all(k):
        return remote(picked.at[k, 0:3], dgot.at[k], ds.at[k], dr.at[k], sibling)

    def d_take(k):
        d_all(k).wait_recv()
        dens_out[:, k * 256 : (k + 1) * 256] = picked[k, pole] + (dgot[k, 0] + dgot[k, 1] + dgot[k, 2])

    def t0_copy(k):
        return remote(zed.at[k, pl.ds((1 - core) * 16, 16)], zcross.at[k], t0s.at[k], t0r.at[k], sibling)

    def t1_send(k):
        t0_copy(k).wait_recv()
        zpart[k] = zed[k, pl.ds(core * 16, 16)] + zcross[k]

        @pl.when(zh == 0)
        def _():
            here = x * 4 + zl
            part = zpart[k, here]
            for p in range(2):
                entry = order[pole * 2 + p]
                part = part + (table[0, entry] * diag[p, 1, k] + table[1, entry] * diag[p, 0, k])
            zpart[k, here] = part

        def send(i, carry):
            at, peer = plane_peer(i)
            remote(zpart.at[k, at], zplane.at[k, i - 1], t1s.at[k], t1r.at[k], peer).start()
            return carry

        lax.fori_loop(1, 16, send, 0)

    def t1_all(k):
        return remote(zpart.at[k, 0:15], zplane.at[k], t1s.at[k], t1r.at[k], sibling)

    def t2_send(k):
        t1_all(k).wait_recv()
        zline[k, z_at] = zpart[k, plane_at] + jnp.sum(zplane[k], axis=0)

        def send(i, carry):
            here = zline.at[k, z_at]
            remote(here, here, t2s.at[k], t2r.at[k], line_peer(i)).start()
            return carry

        lax.fori_loop(1, 8, send, 0)

    def t2_all(k):
        return remote(zline.at[k, 0:7], zline.at[k, 0:7], t2s.at[k], t2r.at[k], sibling)

    def t3_send(k):
        t2_all(k).wait_recv()
        mine = zed_out.at[k, core * 16 + plane_at]
        mine[...] = jnp.sum(zline[k], axis=0)

        def send(i, carry):
            remote(mine, mine, t3s.at[k], t3r.at[k], plane_peer(i)[1]).start()
            return carry

        lax.fori_loop(1, 16, send, 0)

    def t3_all(k):
        here = zed_out.at[k, pl.ds(core * 16, 15)]
        return remote(here, here, t3s.at[k], t3r.at[k], sibling)

    def t4_copy(k):
        here = zed_out.at[k, pl.ds(core * 16, 16)]
        return remote(here, here, t4s.at[k], t4r.at[k], sibling)

    def t4_send(k):
        t3_all(k).wait_recv()
        t4_copy(k).start()

    def own_start(j):
        for d in range(2):
            x_copy(j, 0, d).start()

    def z_next(j):
        z_copy(j - 1).wait_send()
        z_copy(j).start()

    z_copy(0).start()
    own_start(0)
    own_start(1)
    prepare()
    z_next(1)
    x_forward(0, 0)
    own_start(2)
    choose()
    diag_load.wait()
    z_forward(0)
    z_copy(2).start()
    x_forward(1, 0)
    x_forward(0, 1)
    own_start(3)
    z_forward(1)
    z_copy(3).start()
    g_start(0)
    x_forward(2, 0)
    f_wait(0)
    multiply(0)
    x_forward(1, 1)
    c_sum(0)
    z_forward(2)
    x_forward(3, 0)
    g_start(1)
    f_wait(1)
    multiply(1)
    x_forward(2, 1)
    z_forward(3)
    g_mid(0)
    l_mid(0)
    c_sum(1)
    f_wait(2)
    multiply(2)
    x_forward(3, 1)
    l_end(0)
    output(0)
    g_mid(1)
    l_mid(1)
    c_sum(2)
    g_far(0)
    g_end(0)
    zed_early(2)
    f_wait(3)
    multiply(3)
    g_far(1)
    l_end(1)
    output(1)
    t0_copy(0).start()
    d_send(0)
    c_sum(3)
    g_end(1)
    zed_early(3)
    t0_copy(1).start()
    t1_send(0)
    l_mid(2)
    t1_send(1)
    l_end(2)
    output(2)
    t2_send(0)
    t2_send(1)
    l_mid(3)
    t3_send(0)
    t3_send(1)
    l_end(3)
    output(3)
    d_send(1)
    t4_send(0)
    t4_send(1)
    d_take(0)
    for k in range(2):
        t4_copy(k).wait_recv()
    d_take(1)

    for k in range(2):
        for copy in (t0_copy(k), t1_all(k), t2_all(k), t3_all(k), t4_copy(k), d_all(k)):
            copy.wait_send()
    for p in range(2):
        g_own(p, 0, mate).wait_send()

        @pl.when(inner == 1)
        def _(p=p):
            for at in range(1, 5):
                g_own(p, at, mate).wait_send()


    z_copy(NJ - 1).wait_send()
    for j in range(NJ):
        if j in (1, 2):
            z_copy(j).wait_send()
        for h in range(2):
            for d in range(2):
                x_copy(j, h, d).wait_send()
                f_copy(j, h, d).wait_send()
        for d in range(4):
            c_copy(j, d).wait_send()

        @pl.when(inner == 0)
        def _(j=j):
            for d in (3, 2, 1):
                l_copy(j, d - 1, d, mate).wait_send()

        @pl.when(inner == 1)
        def _(j=j):
            for d in (3, 2, 0):
                l_copy(j, 0, d, mate).wait_send()


def main_call(tiles, diag, factor, pattern, owner, anc, order, table):
    vmem = pl.BlockSpec(memory_space=pltpu.VMEM)
    smem = pl.BlockSpec(memory_space=pltpu.SMEM)
    hbm = pl.BlockSpec(memory_space=pl.ANY)
    dma = pltpu.SemaphoreType.DMA
    return pl.pallas_call(
        main_kernel,
        out_shape=(
            jax.ShapeDtypeStruct((2, 2, 64, 512), F32),
            jax.ShapeDtypeStruct((32, 512), F32),
            jax.ShapeDtypeStruct((2, 32, 8, 256), F32),
        ),
        in_specs=[hbm, hbm, vmem, vmem, vmem, smem, smem, smem],
        out_specs=(vmem, vmem, vmem),
        scratch_shapes=[
            pltpu.VMEM((2, 2, 8, 64, 512), F32),
            pltpu.VMEM((2, 2, 2, 8, 256), F32),
            pltpu.VMEM((2, 64, 256), F32),
            pltpu.VMEM((2, 32, 8, 256), F32),
            pltpu.VMEM((2, 16, 8, 256), F32),
            pltpu.VMEM((2, 16, 8, 256), F32),
            pltpu.VMEM((2, 15, 8, 256), F32),
            pltpu.VMEM((2, 8, 8, 256), F32),
            pltpu.VMEM((128, 64), F32),
            pltpu.VMEM((2, 4, 32, 256), F32),
            pltpu.VMEM((2, 3, 32, 256), F32),
            pltpu.VMEM((2, 4, 2, 2, 64, 128), F32),
            pltpu.VMEM((2, 2, 512, 512), BF16),
            pltpu.VMEM((2, 2, 512, 512), BF16),
            pltpu.VMEM((4, 8, 2, 2, 64, 128), F32),
            pltpu.VMEM((2, 512, 512), BF16),
            pltpu.VMEM((2, 512, 512), BF16),
            pltpu.VMEM((4, 8, 2, 2, 64, 128), F32),
            pltpu.VMEM((4, 4, 2, 2, 64, 128), F32),
            pltpu.VMEM((4, 4, 2, 2, 64, 128), F32),
            pltpu.VMEM((4, 5, 2, 2, 64, 128), F32),
            dma, dma,
            dma((NJ,)), dma((NJ,)),
            dma((NJ, 2, 2)), dma((NJ, 2, 2)),
            dma((NJ, 2, 2)), dma((NJ, 2, 2)),
            dma((NJ, 4)), dma((NJ, 4)),
            dma((NJ, 4)), dma((NJ, 5)),
            dma((2, 5)), dma((2, 4)),
            *([dma((2,))] * 12),
        ],
        compiler_params=pltpu.CompilerParams(
            collective_id=0, has_side_effects=True, vmem_limit_bytes=60 * 2**20
        ),
    )(tiles, diag, factor, pattern, owner, anc, order, table)


def finish_kernel(rows, dens, zed, rows_out, dens_out, zed_out):
    rows_out[...] = rows[...]
    dens_out[...] = dens[...]
    zed_out[...] = zed[...]


def finish_call(rows, dens, zed):
    vmem = pl.BlockSpec(memory_space=pltpu.VMEM)
    return pl.pallas_call(
        finish_kernel,
        out_shape=tuple(jax.ShapeDtypeStruct(v.shape, v.dtype) for v in (rows, dens, zed)),
        in_specs=[vmem] * 3,
        out_specs=(vmem,) * 3,
    )(rows, dens, zed)


def shards(tiles, factor, diag, pattern, anc, row_owner, table, order):
    rows, dens, zed = main_call(
        tiles,
        diag.reshape(2, 2, 2, 32, 8, 256),
        factor,
        pattern,
        row_owner.reshape(1, 64),
        anc,
        order,
        table.T,
    )
    rows, dens, zed = finish_call(rows, dens, zed)
    return rows, dens[None], zed.reshape(2, 256, 256)


def solution(mesh):
    placed = (
        P("pole", None, None, "col", "row"),
        P("pole", None, ("row", "col"), None),
        P("pole", None, None, None, None),
        P(),
        P(),
        P(("row", "col"), None),
        P(),
        P(),
    )
    return jax.shard_map(
        shards,
        mesh=mesh,
        in_specs=placed,
        out_specs=(P("pole", None, ("row", "col"), None), P("pole", ("row", "col"), None), P()),
        check_vma=False,
    )
```

```python
import functools

import jax
import jax.numpy as jnp
from jax import lax
from jax.experimental import pallas as pl
from jax.experimental.pallas import tpu as pltpu
from jax.sharding import PartitionSpec as P

MESH = pl.DeviceIdType.MESH
JOBS = ((0, 0, 0, 2), (1, 0, 0, 2), (0, 1, 0, 2), (1, 1, 0, 2))
NJ = len(JOBS)
EARLY = 1
F32, BF16 = jnp.float32, jnp.bfloat16


def split(value):
    high = value.astype(BF16)
    return high, (value - high.astype(F32)).astype(BF16)


def dot(left, right):
    return jnp.dot(left, right, preferred_element_type=F32)


def main_kernel(
    tiles_hbm, diag_hbm, factor, pattern, owner, anc, order, table,
    rows_out, dens_out, zed_out,
    tiles, diag, dens, zed, zcross, zpart, zplane, zline, chosen, picked, dgot, peers_l, a_high, a_low, gath, l_high, l_low, prod, cross, sums, line, tile_sem, diag_sem,
    zs, zr, xs, xr, fs, fr, cs, cr, ls, lr,
    gs, gr, t0s, t0r, t1s, t1r, t2s, t2r, t3s, t3r, t4s, t4r, ds, dr,
):
    pole, row, col = lax.axis_index("pole"), lax.axis_index("row"), lax.axis_index("col")
    zl, core = row // 2, row % 2
    x, zh = col // 2, col % 2
    half = zl // 2
    inner = zl + half * (3 - 2 * zl)
    other_col = x * 2 + 1 - zh
    right_x, left_x = (x + 1) % 4, (x + 3) % 4

    partner = (pole, row, other_col)
    right = (pole, row, right_x * 2 + zh)
    left = (pole, row, left_x * 2 + zh)
    sibling = (pole, zl * 2 + 1 - core, col)
    mate = (pole, (1 - inner + half * (1 + 2 * inner)) * 2 + core, col)
    across = (pole, (3 - zl) * 2 + core, col)

    load = pltpu.make_async_copy(tiles_hbm, tiles, tile_sem)
    load.start()

    plane_at = pole * 4 + x
    z_at = zh * 4 + zl
    diag_load = pltpu.make_async_copy(
        diag_hbm.at[:, :, :, core * 16 + x * 4 + zl], diag, diag_sem
    )
    diag_load.start()

    def plane_peer(i):
        at = (plane_at + i) % 16
        return at, (at // 4, row, (at % 4) * 2 + zh)

    def line_peer(i):
        at = (z_at + i) % 8
        return (pole, (at % 4) * 2 + core, x * 2 + at // 4)

    barrier = pltpu.get_barrier_semaphore()

    def greet_plane(i, carry):
        pl.semaphore_signal(barrier, inc=1, device_id=plane_peer(i)[1], device_id_type=MESH)
        return carry

    def greet_line(i, carry):
        pl.semaphore_signal(barrier, inc=1, device_id=line_peer(i), device_id_type=MESH)
        return carry

    lax.fori_loop(1, 16, greet_plane, 0)
    lax.fori_loop(1, 8, greet_line, 0)
    pl.semaphore_signal(barrier, inc=1, device_id=sibling, device_id_type=MESH)

    block = row * 8 + col
    keeps = [anc[k, block].astype(F32) for k in range(2)]
    zed[...] = jnp.zeros_like(zed)
    for p in range(2):
        for k in range(2):
            for h in range(2):
                first = k * 256 + h * 128
                gath[k * 2 + p, col, h] = factor[p, :, :, first : first + 128] * keeps[k]

    pl.semaphore_wait(barrier, 23)

    def remote(src, dst, send, recv, peer):
        return pltpu.make_async_remote_copy(
            src_ref=src, dst_ref=dst, send_sem=send, recv_sem=recv, device_id=peer, device_id_type=MESH
        )

    def view(ref, j, *at):
        p, k, first, count = JOBS[j]
        return ref.at[(k * 2 + p, *at, pl.ds(first, count))]

    def half_view(j, slot, d):
        p, k, first, count = JOBS[j]
        return gath.at[k * 2 + p, slot, d] if count == 2 else gath.at[k * 2 + p, slot, first, d]

    def z_copy(j):
        return remote(view(gath, j, col), view(gath, j, col), zs.at[j], zr.at[j], partner)

    def z_recv(j):
        return remote(view(gath, j, other_col), view(gath, j, other_col), zs.at[j], zr.at[j], partner)

    def x_copy(j, h, d):
        slot = col if h == 0 else other_col
        peer = right if d == 0 else left
        return remote(view(gath, j, slot), view(gath, j, slot), xs.at[j, h, d], xr.at[j, h, d], peer)

    def x_slot(h, shift):
        half_of = zh if h == 0 else 1 - zh
        return ((x + shift) % 4) * 2 + half_of

    def x_recv(j, h, d):
        slot = x_slot(h, 3 if d == 0 else 1)
        return remote(view(gath, j, slot), view(gath, j, slot), xs.at[j, h, d], xr.at[j, h, d], right)

    def f_copy(j, h, d):
        slot = x_slot(h, 3 if d == 0 else 1)
        peer = right if d == 0 else left
        return remote(half_view(j, slot, d), half_view(j, slot, d), fs.at[j, h, d], fr.at[j, h, d], peer)

    def f_recv(j, h, d):
        slot = x_slot(h, 2)
        return remote(half_view(j, slot, d), half_view(j, slot, d), fs.at[j, h, d], fr.at[j, h, d], right)

    def z_forward(j):
        z_recv(j).wait_recv()
        for d in range(2):
            x_copy(j, 1, d).start()

    def x_forward(j, h):
        for d in range(2):
            x_recv(j, h, d).wait_recv()
            f_copy(j, h, d).start()

    def f_wait(j):
        for h in range(2):
            for d in range(2):
                f_recv(j, h, d).wait_recv()

    def prepare():
        load.wait()
        expand = (
            lax.broadcasted_iota(jnp.int32, (64, 512), 0)
            == row * 8 + lax.broadcasted_iota(jnp.int32, (64, 512), 1) // 64
        ).astype(BF16)
        tile_rows = jnp.concatenate(
            [pattern[pl.ds(g * 8 + col, 1), :] for g in range(8)], axis=0
        ).astype(F32).astype(BF16)
        keep_cols = dot(tile_rows, expand)
        for g in range(8):
            mask = keep_cols[g : g + 1, :]

            def one(i, carry, g=g, mask=mask):
                p, part = i // 2, i % 2
                high, low = split(tiles[p, part, g] * mask)
                a_high[p, part, g * 64 : (g + 1) * 64] = high
                a_low[p, part, g * 64 : (g + 1) * 64] = low
                return carry

            lax.fori_loop(0, 4, one, 0)

    def multiply(j):
        p, k, first, count = JOBS[j]
        b = k * 2 + p

        def halves(c, carry):
            at = pl.ds(pl.multiple_of(c * 64, 64), 64)
            for h in range(first, first + count):
                for part in range(2):
                    high, low = split(gath[b, c, h, part])
                    same = slice(h * 256 + part * 128, h * 256 + part * 128 + 128)
                    turned = slice(h * 256 + 128 - part * 128, h * 256 + 256 - part * 128)
                    l_high[0, at, same] = high
                    l_low[0, at, same] = low
                    l_high[1, at, turned] = -high if part else high
                    l_low[1, at, turned] = -low if part else low
            return carry

        lax.fori_loop(0, 8, halves, 0)

        def one(h, carry):
            at = pl.ds(pl.multiple_of(h * 256, 256), 256)
            total = None
            for part in range(2):
                bh, bl = l_high[part, :, at], l_low[part, :, at]
                ah, al = a_high[p, part], a_low[p, part]
                term = dot(ah, bh) + (dot(ah, bl) + dot(al, bh))
                total = term if total is None else total + term
            for g in range(8):
                rows = total[g * 64 : (g + 1) * 64]
                prod[b, g, h, 0] = rows[:, :128]
                prod[b, g, h, 1] = rows[:, 128:]
            return carry

        lax.fori_loop(first, first + count, one, 0)
        for d in range(4):
            c_copy(j, d).start()

    def c_copy(j, d):
        return remote(
            view(prod, j, d * 2 + 1 - core), view(cross, j, d), cs.at[j, d], cr.at[j, d], sibling
        )

    def at_line(d):
        return d + half * (3 - 2 * d)

    def l_copy(j, slot, d, peer):
        return remote(view(sums, j, d), view(line, j, slot), ls.at[j, d], lr.at[j, slot], peer)

    def l_wait(j, slot):
        l_copy(j, slot, 0, mate).wait_recv()
        return view(line, j, slot)[...]

    def c_sum(j):
        for d in (3, 2, 1, 0):
            place = at_line(d)
            remote(
                view(prod, j, 0), view(cross, j, place), cs.at[j, d], cr.at[j, place], sibling
            ).wait_recv()
            view(sums, j, d)[...] = view(prod, j, place * 2 + core)[...] + view(cross, j, place)[...]
            if d > 0:

                @pl.when(inner == 0)
                def _(d=d):
                    l_copy(j, d - 1, d, mate).start()

    def l_mid(j):
        @pl.when(inner == 1)
        def _():
            for d in (3, 2):
                here = view(sums, j, d)
                here[...] = here[...] + l_wait(j, d - 1)
                l_copy(j, 6 - d, d, across).start()

    def l_end(j):
        @pl.when(inner == 1)
        def _():
            here = view(sums, j, 0)
            here[...] = here[...] + l_wait(j, 3)
            l_copy(j, 3, 0, mate).start()
            here = view(sums, j, 1)
            here[...] = here[...] + (l_wait(j, 0) + l_wait(j, 4))

        @pl.when(inner == 0)
        def _():
            here = view(sums, j, 0)
            here[...] = here[...] + l_wait(j, 3)

    def output(j):
        p, k, first, count = JOBS[j]
        entry = order[pole * 2 + p]
        wr, wi = table[0, entry], table[1, entry]
        done = view(sums, j, inner)[...] * keeps[k]
        for i in range(count):
            lanes = slice((first + i) * 128, (first + i + 1) * 128)
            rows_out[p, :, :, k * 256 + lanes.start : k * 256 + lanes.stop] = done[i]
            density = wr * done[i, 1] + wi * done[i, 0]
            if p == 0:
                dens[k, :, lanes] = density
            else:
                dens[k, :, lanes] += density
        if k != EARLY:
            zed_add(j, weighted(gath[k * 2 + p, col], p), done)

    def weighted(block, p):
        entry = order[pole * 2 + p]
        wr, wi = table[0, entry], table[1, entry]
        panels = [
            jnp.concatenate(
                [wr * block[h, 1] + wi * block[h, 0], wr * block[h, 0] - wi * block[h, 1]], axis=0
            )
            for h in range(2)
        ]
        return jnp.concatenate(panels, axis=1)

    def zed_add(j, left_side, values):
        p, k, first, count = JOBS[j]
        for i in range(count):
            product = lax.dot_general(
                left_side, values[i].reshape(128, 128), (((0,), (0,)), ((), ())),
                precision=lax.Precision.HIGHEST, preferred_element_type=F32,
            ).reshape(32, 8, 128)
            zed[k, :, :, (first + i) * 128 : (first + i + 1) * 128] -= product

    def g_copy(p, source, place, at, peer):
        return remote(source, peers_l.at[p, place], gs.at[p, at], gr.at[p, place], peer)

    def g_own(p, at, peer):
        return g_copy(p, gath.at[2 + p, col], zl, at, peer)

    def g_wait(p, d):
        g_copy(p, gath.at[2 + p, col], at_line(d), 0, mate).wait_recv()

    def g_pass(p, d, at, peer):
        place = at_line(d)
        return g_copy(p, peers_l.at[p, place], place, at, peer)

    def g_start(p):
        peers_l[p, zl] = gath[2 + p, col]

        @pl.when(inner == 0)
        def _():
            g_own(p, 0, mate).start()

        @pl.when(inner == 1)
        def _():
            g_own(p, 0, across).start()
            g_own(p, 1, mate).start()

    def g_mid(p):
        @pl.when(inner == 1)
        def _():
            g_wait(p, 0)
            g_pass(p, 0, 2, across).start()
            g_wait(p, 2)
            g_pass(p, 2, 3, mate).start()

    def g_far(p):
        @pl.when(inner == 1)
        def _():
            g_wait(p, 3)
            g_pass(p, 3, 4, mate).start()

    def g_end(p):
        @pl.when(inner == 0)
        def _():
            for d in (1, 2, 3):
                g_wait(p, d)

    def zed_early(j):
        p = JOBS[j][0]

        def one(d, carry):
            zed_add(j, weighted(peers_l[p, at_line(d)], p), view(sums, j, d)[...])
            return carry

        lax.fori_loop(0, 4, one, 0)

    def choose():
        lines = lax.broadcasted_iota(jnp.int32, (128, 64), 0)
        hot = (owner[...] == lines // 32).astype(F32)
        before = (
            lax.broadcasted_iota(jnp.int32, (64, 64), 0) < lax.broadcasted_iota(jnp.int32, (64, 64), 1)
        ).astype(BF16)
        rank = dot(hot.astype(BF16), before)
        chosen[...] = jnp.where(rank == (lines % 32).astype(F32), hot, 0.0)

    def d_copy(k, i):
        to = (pole + i) % 4
        return remote(picked.at[k, to], dgot.at[k, i - 1], ds.at[k], dr.at[k], (to, row, col))

    def d_send(k):
        picked[k] = lax.dot_general(
            chosen[...], dens[k], (((1,), (0,)), ((), ())),
            precision=lax.Precision.HIGHEST, preferred_element_type=F32,
        ).reshape(4, 32, 256)
        for i in range(1, 4):
            d_copy(k, i).start()

    def d_all(k):
        return remote(picked.at[k, 0:3], dgot.at[k], ds.at[k], dr.at[k], sibling)

    def d_take(k):
        d_all(k).wait_recv()
        dens_out[:, k * 256 : (k + 1) * 256] = picked[k, pole] + (dgot[k, 0] + dgot[k, 1] + dgot[k, 2])

    def t0_copy(k):
        return remote(zed.at[k, pl.ds((1 - core) * 16, 16)], zcross.at[k], t0s.at[k], t0r.at[k], sibling)

    def t1_send(k):
        t0_copy(k).wait_recv()
        zpart[k] = zed[k, pl.ds(core * 16, 16)] + zcross[k]

        @pl.when(zh == 0)
        def _():
            here = x * 4 + zl
            part = zpart[k, here]
            for p in range(2):
                entry = order[pole * 2 + p]
                part = part + (table[0, entry] * diag[p, 1, k] + table[1, entry] * diag[p, 0, k])
            zpart[k, here] = part

        def send(i, carry):
            at, peer = plane_peer(i)
            remote(zpart.at[k, at], zplane.at[k, i - 1], t1s.at[k], t1r.at[k], peer).start()
            return carry

        lax.fori_loop(1, 16, send, 0)

    def t1_all(k):
        return remote(zpart.at[k, 0:15], zplane.at[k], t1s.at[k], t1r.at[k], sibling)

    def t2_send(k):
        t1_all(k).wait_recv()
        zline[k, z_at] = zpart[k, plane_at] + jnp.sum(zplane[k], axis=0)

        def send(i, carry):
            here = zline.at[k, z_at]
            remote(here, here, t2s.at[k], t2r.at[k], line_peer(i)).start()
            return carry

        lax.fori_loop(1, 8, send, 0)

    def t2_all(k):
        return remote(zline.at[k, 0:7], zline.at[k, 0:7], t2s.at[k], t2r.at[k], sibling)

    def t3_send(k):
        t2_all(k).wait_recv()
        mine = zed_out.at[k, core * 16 + plane_at]
        mine[...] = jnp.sum(zline[k], axis=0)

        def send(i, carry):
            remote(mine, mine, t3s.at[k], t3r.at[k], plane_peer(i)[1]).start()
            return carry

        lax.fori_loop(1, 16, send, 0)

    def t3_all(k):
        here = zed_out.at[k, pl.ds(core * 16, 15)]
        return remote(here, here, t3s.at[k], t3r.at[k], sibling)

    def t4_copy(k):
        here = zed_out.at[k, pl.ds(core * 16, 16)]
        return remote(here, here, t4s.at[k], t4r.at[k], sibling)

    def t4_send(k):
        t3_all(k).wait_recv()
        t4_copy(k).start()

    def own_start(j):
        for d in range(2):
            x_copy(j, 0, d).start()

    def z_next(j):
        z_copy(j - 1).wait_send()
        z_copy(j).start()

    z_copy(0).start()
    own_start(0)
    own_start(1)
    prepare()
    z_next(1)
    x_forward(0, 0)
    own_start(2)
    choose()
    diag_load.wait()
    z_forward(0)
    z_copy(2).start()
    x_forward(1, 0)
    x_forward(0, 1)
    own_start(3)
    z_forward(1)
    z_copy(3).start()
    g_start(0)
    x_forward(2, 0)
    f_wait(0)
    multiply(0)
    x_forward(1, 1)
    c_sum(0)
    z_forward(2)
    x_forward(3, 0)
    g_start(1)
    f_wait(1)
    multiply(1)
    x_forward(2, 1)
    z_forward(3)
    g_mid(0)
    l_mid(0)
    c_sum(1)
    f_wait(2)
    multiply(2)
    x_forward(3, 1)
    l_end(0)
    output(0)
    g_mid(1)
    l_mid(1)
    c_sum(2)
    g_far(0)
    g_end(0)
    zed_early(2)
    f_wait(3)
    multiply(3)
    g_far(1)
    l_end(1)
    output(1)
    t0_copy(0).start()
    d_send(0)
    l_mid(2)
    c_sum(3)
    g_end(1)
    zed_early(3)
    t0_copy(1).start()
    t1_send(0)
    t1_send(1)
    l_end(2)
    output(2)
    t2_send(0)
    t2_send(1)
    l_mid(3)
    t3_send(0)
    t3_send(1)
    l_end(3)
    output(3)
    d_send(1)
    t4_send(0)
    t4_send(1)
    d_take(0)
    for k in range(2):
        t4_copy(k).wait_recv()
    d_take(1)

    for k in range(2):
        for copy in (t0_copy(k), t1_all(k), t2_all(k), t3_all(k), t4_copy(k), d_all(k)):
            copy.wait_send()
    for p in range(2):
        g_own(p, 0, mate).wait_send()

        @pl.when(inner == 1)
        def _(p=p):
            for at in range(1, 5):
                g_own(p, at, mate).wait_send()


    z_copy(NJ - 1).wait_send()
    for j in range(NJ):
        if j in (1, 2):
            z_copy(j).wait_send()
        for h in range(2):
            for d in range(2):
                x_copy(j, h, d).wait_send()
                f_copy(j, h, d).wait_send()
        for d in range(4):
            c_copy(j, d).wait_send()

        @pl.when(inner == 0)
        def _(j=j):
            for d in (3, 2, 1):
                l_copy(j, d - 1, d, mate).wait_send()

        @pl.when(inner == 1)
        def _(j=j):
            for d in (3, 2, 0):
                l_copy(j, 0, d, mate).wait_send()


def main_call(tiles, diag, factor, pattern, owner, anc, order, table):
    vmem = pl.BlockSpec(memory_space=pltpu.VMEM)
    smem = pl.BlockSpec(memory_space=pltpu.SMEM)
    hbm = pl.BlockSpec(memory_space=pl.ANY)
    dma = pltpu.SemaphoreType.DMA
    return pl.pallas_call(
        main_kernel,
        out_shape=(
            jax.ShapeDtypeStruct((2, 2, 64, 512), F32),
            jax.ShapeDtypeStruct((32, 512), F32),
            jax.ShapeDtypeStruct((2, 32, 8, 256), F32),
        ),
        in_specs=[hbm, hbm, vmem, vmem, vmem, smem, smem, smem],
        out_specs=(vmem, vmem, vmem),
        scratch_shapes=[
            pltpu.VMEM((2, 2, 8, 64, 512), F32),
            pltpu.VMEM((2, 2, 2, 8, 256), F32),
            pltpu.VMEM((2, 64, 256), F32),
            pltpu.VMEM((2, 32, 8, 256), F32),
            pltpu.VMEM((2, 16, 8, 256), F32),
            pltpu.VMEM((2, 16, 8, 256), F32),
            pltpu.VMEM((2, 15, 8, 256), F32),
            pltpu.VMEM((2, 8, 8, 256), F32),
            pltpu.VMEM((128, 64), F32),
            pltpu.VMEM((2, 4, 32, 256), F32),
            pltpu.VMEM((2, 3, 32, 256), F32),
            pltpu.VMEM((2, 4, 2, 2, 64, 128), F32),
            pltpu.VMEM((2, 2, 512, 512), BF16),
            pltpu.VMEM((2, 2, 512, 512), BF16),
            pltpu.VMEM((4, 8, 2, 2, 64, 128), F32),
            pltpu.VMEM((2, 512, 512), BF16),
            pltpu.VMEM((2, 512, 512), BF16),
            pltpu.VMEM((4, 8, 2, 2, 64, 128), F32),
            pltpu.VMEM((4, 4, 2, 2, 64, 128), F32),
            pltpu.VMEM((4, 4, 2, 2, 64, 128), F32),
            pltpu.VMEM((4, 5, 2, 2, 64, 128), F32),
            dma, dma,
            dma((NJ,)), dma((NJ,)),
            dma((NJ, 2, 2)), dma((NJ, 2, 2)),
            dma((NJ, 2, 2)), dma((NJ, 2, 2)),
            dma((NJ, 4)), dma((NJ, 4)),
            dma((NJ, 4)), dma((NJ, 5)),
            dma((2, 5)), dma((2, 4)),
            *([dma((2,))] * 12),
        ],
        compiler_params=pltpu.CompilerParams(
            collective_id=0, has_side_effects=True, vmem_limit_bytes=60 * 2**20
        ),
    )(tiles, diag, factor, pattern, owner, anc, order, table)


def finish_kernel(rows, dens, zed, rows_out, dens_out, zed_out):
    rows_out[...] = rows[...]
    dens_out[...] = dens[...]
    zed_out[...] = zed[...]


def finish_call(rows, dens, zed):
    vmem = pl.BlockSpec(memory_space=pltpu.VMEM)
    return pl.pallas_call(
        finish_kernel,
        out_shape=tuple(jax.ShapeDtypeStruct(v.shape, v.dtype) for v in (rows, dens, zed)),
        in_specs=[vmem] * 3,
        out_specs=(vmem,) * 3,
    )(rows, dens, zed)


def shards(tiles, factor, diag, pattern, anc, row_owner, table, order):
    rows, dens, zed = main_call(
        tiles,
        diag.reshape(2, 2, 2, 32, 8, 256),
        factor,
        pattern,
        row_owner.reshape(1, 64),
        anc,
        order,
        table.T,
    )
    rows, dens, zed = finish_call(rows, dens, zed)
    return rows, dens[None], zed.reshape(2, 256, 256)


def solution(mesh):
    placed = (
        P("pole", None, None, "col", "row"),
        P("pole", None, ("row", "col"), None),
        P("pole", None, None, None, None),
        P(),
        P(),
        P(("row", "col"), None),
        P(),
        P(),
    )
    return jax.shard_map(
        shards,
        mesh=mesh,
        in_specs=placed,
        out_specs=(P("pole", None, ("row", "col"), None), P("pole", ("row", "col"), None), P()),
        check_vma=False,
    )
```
